256 devices in a mesh: ctx: 64 (over z, y, x_hi), tp: 4 (over x_lo, core).
Axes of the slice: x: 4 (x_hi: 2, x_lo: 2; x = x_hi * 2 + x_lo), y: 4, z: 8, core: 2. Of those that a mesh axis runs over, the one named last changes fastest.
Arguments:
- features: bfloat16 [3, 16384, 8192], P(None, 'ctx', 'tp'), may hold values from -6 to 6
- short_weight: float32 [3, 3, 8192], P(None, None, 'tp'), may hold values from -2.5 to 2.5
- filters: float32 [512, 16384], P(('tp', 'ctx')), may hold values from -2 to 2, as said below
- out_weight: bfloat16 [8192, 4096], P(('tp', 'ctx')), may hold values from -0.0625 to 0.0625
Outputs:
- projected: bfloat16 [16384, 4096], P('ctx', 'tp')
The draws below stay inside these ranges and needn't reach their ends.
Inputs may be any that keep to these rules, and one draw needn't show every extreme that they name: `filters`: real values.
All inputs are finite; a program needn't handle non-finite values.
Results may differ from the reference program's by a relative error of at most 0.015.
Values may be sent and summed in bfloat16 or wider, within the bound.
No kernel may reach another device: no remote copies, remote signals or barrier semaphores. Data moves between devices by JAX's collectives and lax.ppermute only.
A program may use at most 128 MiB of HBM per device.

```python
import math
import jax
import jax.numpy as jnp
from jax import lax

D = 8192
DW = 4096
GROUP = 16
KERNEL = 3
L = 16384
G = 512


def draw_filters(key, part):
    key_rate = jax.random.fold_in(key, 11)
    key_noise = jax.random.fold_in(key, 23)
    lag_index = jnp.arange(L, dtype=jnp.float32)[None, :]
    log_rate = jax.random.uniform(key_rate, (G, 1), jnp.float32, math.log(0.3 / L), math.log(1.0 / 12.0))
    rough_part = jnp.clip(jax.random.normal(key_noise, (G, L), jnp.float32), -5.0, 5.0)
    decay_rate = jnp.exp(log_rate)
    norm_factor = jnp.sqrt((1.0 - jnp.exp(-2.0 * decay_rate)) / (1.0 - jnp.exp(-2.0 * decay_rate * L)))
    return rough_part * jnp.exp(-decay_rate * lag_index) * norm_factor


def block_scale(stream_key, extent, cuts, smallest, high):
    level, own = 1.0, jax.random.fold_in(stream_key, 6)
    for position, parts in cuts:
        heights = jnp.exp(jax.random.uniform(jax.random.fold_in(own, position), (parts,), jnp.float32, smallest / len(cuts), high / len(cuts)))
        level = level * jnp.repeat(heights, extent[position] // parts).reshape([-1 if axis == position else 1 for axis in range(len(extent))])
    return level


def gaussian(stream_key, shape, width, most, cuts=(), held_as=jnp.bfloat16):
    values = width * jax.random.normal(stream_key, shape, jnp.float32)
    if cuts:
        values = values * block_scale(stream_key, shape, cuts, -0.22, 0.18)
    return jnp.clip(values, -most, most).astype(held_as)


def setup_inputs(seed: int = 0) -> dict:
    arg_keys = jax.random.split(jax.random.key(seed), 5)
    return {
        "features": gaussian(arg_keys[0], (3, L, D), 1.0, 6.0, ((1, 64), (2, 4))),
        "short_weight": gaussian(arg_keys[1], (3, KERNEL, D), 0.4, 2.5, ((2, 4),), jnp.float32),
        "filters": draw_filters(jax.random.fold_in(arg_keys[4], 71), 0),
        "out_weight": gaussian(arg_keys[3], (D, DW), D ** -0.5, 0.0625, ((0, 256),)),
    }


def reference(features, short_weight, filters, out_weight):
    padded = jnp.pad(features, ((0, 0), (KERNEL - 1, 0), (0, 0)))
    mixture = jnp.zeros(features.shape, jnp.float32)
    for offset in range(KERNEL):
        mixture = mixture + padded[:, offset:offset + L, :].astype(jnp.float32) * short_weight[:, offset, None, :].astype(jnp.float32)
    featurized = mixture.astype(jnp.bfloat16)
    product = (featurized[1].astype(jnp.float32) * featurized[2].astype(jnp.float32)).astype(jnp.bfloat16)
    grouped = product.astype(jnp.float32).T.reshape(G, GROUP, L)

    def one_group(operands):
        signal, kernel = operands
        spectrum = jnp.fft.rfft(signal, n=2 * L, axis=-1) * jnp.fft.rfft(kernel, n=2 * L)[None, :]
        return jnp.fft.irfft(spectrum, n=2 * L, axis=-1)[:, :L]

    convolved = lax.map(one_group, (grouped, filters))
    convolved = convolved.reshape(D, L).T.astype(jnp.bfloat16)
    gated_out = (featurized[0].astype(jnp.float32) * convolved.astype(jnp.float32)).astype(jnp.bfloat16)
    return jnp.dot(gated_out, out_weight, preferred_element_type=jnp.float32).astype(jnp.bfloat16)
```

```python
import functools

import jax
import jax.numpy as jnp
from jax import lax
from jax.experimental import pallas as pl
from jax.experimental.pallas import tpu as pltpu
from jax.sharding import Mesh, PartitionSpec as P

CTX = ("z", "y", "xh")
RING = ("xh", "xl")
F32, BF16 = jnp.float32, jnp.bfloat16
TOK = 256
WIDE = 8
VMEM = 56 * 1024 * 1024


def featurize_kernel(first_ref, x_ref, halo_ref, w_ref, prod_ref, gate_ref):
    rows = lax.broadcasted_iota(jnp.int32, x_ref.shape[1:], 0)
    live = first_ref[0] != 0

    def one(i):
        x = x_ref[i].astype(F32)
        halo = jnp.where(live, halo_ref[i].astype(F32), 0.0)
        x1 = jnp.where(rows == 0, halo[1:2], pltpu.roll(x, 1, 0))
        x2 = jnp.where(rows == 0, halo[0:1], pltpu.roll(x1, 1, 0))
        taps = w_ref[i]
        mix = x2 * taps[0:1] + x1 * taps[1:2] + x * taps[2:3]
        return mix.astype(BF16).astype(F32)

    prod_ref[...] = (one(1) * one(2)).T.astype(BF16)
    gate_ref[...] = one(0).T.astype(BF16)


def featurize(first, features, halo, taps, width=256):
    _, tok, chans = features.shape
    out = jax.ShapeDtypeStruct((chans, tok), BF16)
    return pl.pallas_call(
        featurize_kernel,
        grid=(chans // width,),
        in_specs=[
            pl.BlockSpec(memory_space=pltpu.SMEM),
            pl.BlockSpec((3, tok, width), lambda i: (0, 0, i)),
            pl.BlockSpec((3, 2, width), lambda i: (0, 0, i)),
            pl.BlockSpec((3, 3, width), lambda i: (0, 0, i)),
        ],
        out_specs=[pl.BlockSpec((width, tok), lambda i: (i, 0))] * 2,
        out_shape=[out, out],
        name="featurize",
    )(first, features, halo, taps)


def toeplitz_kernel(h_ref, t_ref):
    step = pl.program_id(1)
    span = TOK * WIDE
    base = pl.multiple_of(step * span, span)
    lags = h_ref[0, :, pl.ds(base, span + TOK)]
    strip = 16
    for i in range(TOK // strip):
        wide = jnp.broadcast_to(lags, (strip, span + TOK))
        slid = pltpu.roll(wide, i * strip, 1, stride=1, stride_axis=0)
        slid = slid.astype(BF16)
        for k in range(WIDE):
            t_ref[0, k, i * strip : (i + 1) * strip, :] = slid[:, (k + 1) * TOK : (k + 2) * TOK]


def toeplitz(filters):
    groups, length = filters.shape
    blocks = length // TOK
    padded = jnp.pad(filters, ((0, 0), (TOK, 0)))[:, None, :]
    return pl.pallas_call(
        toeplitz_kernel,
        grid=(groups, blocks // WIDE),
        in_specs=[pl.BlockSpec((1, 1, length + TOK), lambda g, s: (g, 0, 0))],
        out_specs=pl.BlockSpec((1, WIDE, TOK, TOK), lambda g, s: (g, s, 0, 0)),
        out_shape=jax.ShapeDtypeStruct((groups, blocks, TOK, TOK), BF16),
        cost_estimate=pl.CostEstimate(flops=0, bytes_accessed=48 * 2**20, transcendentals=0),
        name="toeplitz",
    )(padded)


def conv_kernel(per_group, x_ref, t_ref, y_ref, wide_ref, acc_ref):
    step = pl.program_id(1)
    blocks = x_ref.shape[0]
    rows = blocks * per_group

    @pl.when(step == 0)
    def _():
        x = x_ref[...].reshape(rows, TOK)
        for j in range(WIDE):
            lead = j * per_group
            if lead:
                wide_ref[0:lead, j * TOK : (j + 1) * TOK] = jnp.zeros((lead, TOK), BF16)
            wide_ref[lead:, j * TOK : (j + 1) * TOK] = x[: rows - lead]

    t = t_ref[0].reshape(WIDE * TOK, TOK)
    for s in range(blocks // WIDE):

        @pl.when(step == s)
        def _():
            lead = s * WIDE * per_group
            part = jnp.dot(wide_ref[0 : rows - lead, :], t, preferred_element_type=F32)
            if s == 0:
                acc_ref[...] = part
            else:
                acc_ref[lead:, :] += part

    @pl.when(step == blocks // WIDE - 1)
    def _():
        y_ref[...] = acc_ref[...].astype(BF16).reshape(y_ref.shape)


def long_conv(x, t):
    blocks, chans, tok = x.shape
    groups = t.shape[0]
    per_group = chans // groups
    return pl.pallas_call(
        functools.partial(conv_kernel, per_group),
        grid=(groups, blocks // WIDE),
        in_specs=[
            pl.BlockSpec((blocks, per_group, tok), lambda g, s: (0, g, 0)),
            pl.BlockSpec((1, WIDE, TOK, TOK), lambda g, s: (g, s, 0, 0)),
        ],
        out_specs=pl.BlockSpec((blocks, per_group, tok), lambda g, s: (0, g, 0)),
        out_shape=jax.ShapeDtypeStruct(x.shape, BF16),
        scratch_shapes=[
            pltpu.VMEM((blocks * per_group, WIDE * TOK), BF16),
            pltpu.VMEM((blocks * per_group, TOK), F32),
        ],
        compiler_params=pltpu.CompilerParams(vmem_limit_bytes=VMEM),
        cost_estimate=pl.CostEstimate(
            flops=chans * blocks * blocks * tok * tok, bytes_accessed=20 * 2**20, transcendentals=0
        ),
        name="long_conv",
    )(x, t)


def gate_kernel(conv_ref, gate_ref, out_ref):
    gated = conv_ref[...].astype(F32) * gate_ref[...].astype(F32)
    chans = conv_ref.shape[0] * conv_ref.shape[2]
    for x in range(2):
        part = gated[:, x].astype(BF16).astype(F32).reshape(chans, TOK)
        out_ref[x] = part.T.astype(BF16)


def gating(conv, gate):
    srcs, halves, chans, tok = conv.shape
    group = 8
    return pl.pallas_call(
        gate_kernel,
        grid=(srcs // group,),
        in_specs=[pl.BlockSpec((group, halves, chans, tok), lambda i: (i, 0, 0, 0))] * 2,
        out_specs=pl.BlockSpec((halves, tok, group * chans), lambda i: (0, 0, i)),
        out_shape=jax.ShapeDtypeStruct((halves, tok, srcs * chans), BF16),
        name="gating",
    )(conv, gate)


def project_kernel(where_ref, a_ref, w_ref, *refs):
    del where_ref
    a = a_ref[0]
    part = jnp.dot(a, w_ref[...], preferred_element_type=F32)
    if len(refs) == 2:
        part = part + refs[0][0].astype(F32)
    refs[-1][0] = part.astype(BF16)


def project(where, a, w, added=None):
    halves, tok, chans = a.shape
    width = w.shape[1] // 4
    block = pl.BlockSpec((1, tok, width), lambda r, s: (r, 0, 0))
    return pl.pallas_call(
        project_kernel,
        grid_spec=pltpu.PrefetchScalarGridSpec(
            num_scalar_prefetch=1,
            grid=(4,),
            in_specs=[
                pl.BlockSpec((1, tok, chans), lambda r, s: (s[0, r], 0, 0)),
                pl.BlockSpec((chans, width), lambda r, s: (0, s[1, r])),
            ]
            + ([block] if added is not None else []),
            out_specs=block,
        ),
        out_shape=jax.ShapeDtypeStruct((4, tok, width), BF16),
        compiler_params=pltpu.CompilerParams(vmem_limit_bytes=VMEM),
        name="project",
    )(where, a, w, *([added] if added is not None else []))


def on_device(features, short_weight, filters, out_weight):
    tok, chans = features.shape[1:]
    rim = features[:, tok - 2 :, :]
    ctx_size = lax.axis_size(CTX)
    halo = lax.ppermute(rim, CTX, [(i, (i + 1) % ctx_size) for i in range(ctx_size)])
    live = jnp.where(lax.axis_index(CTX) == 0, 0, 1).astype(jnp.int32)[None]
    weights = lax.all_gather(out_weight, ("z", "y"), axis=0, tiled=True)
    product, gate = featurize(live, features, halo, short_weight)
    mine = chans // ctx_size
    series = lax.all_to_all(
        product.reshape(ctx_size, mine, tok), CTX, split_axis=0, concat_axis=0, tiled=True
    )
    blocks = toeplitz(filters)
    xh, xl, core = lax.axis_index("xh"), lax.axis_index("xl"), lax.axis_index("core")
    gate = gate.reshape(ctx_size // 2, 2, mine, tok)
    own = lax.dynamic_index_in_dim(gate, xh, 1, keepdims=False)
    other = lax.dynamic_index_in_dim(gate, 1 - xh, 1, keepdims=False)
    other = lax.ppermute(other, "xh", [(0, 1), (1, 0)])
    gates = jnp.where(xh == 0, jnp.stack([own, other], 1), jnp.stack([other, own], 1))

    convolved = long_conv(series, blocks)
    convolved = convolved.reshape(ctx_size // 2, 2, mine, tok)
    back = lax.all_to_all(convolved, ("z", "y"), split_axis=0, concat_axis=0, tiled=True)
    gated = gating(back, gates)

    place = xh * 2 + xl
    there = (place + jnp.arange(4, dtype=jnp.int32)) % 4
    half, lane = there // 2, there % 2
    out_block = jnp.stack([half, lane * 2 + (1 - core)]).astype(jnp.int32)
    own_block = jnp.stack([half, lane * 2 + core]).astype(jnp.int32)
    passed = project(out_block, gated, weights)
    passed = lax.ppermute(passed, "core", [(0, 1), (1, 0)])
    sums = project(own_block, gated, weights, passed)
    total = sums[0].astype(F32)
    for r in range(1, 4):
        got = lax.ppermute(sums[r], RING, [(i, (i + r) % 4) for i in range(4)])
        total = total + got.astype(F32)
    return total.astype(BF16)


def solution(mesh):
    fine = Mesh(mesh.devices.reshape(8, 4, 2, 2, 2), ("z", "y", "xh", "xl", "core"))
    tp = ("xl", "core")
    in_specs = (
        P(None, CTX, tp),
        P(None, None, tp),
        P(tp + CTX, None),
        P(tp + CTX, None),
    )
    return jax.shard_map(
        on_device, mesh=fine, in_specs=in_specs, out_specs=P(CTX, tp), check_vma=False
    )
```

```python
import functools

import jax
import jax.numpy as jnp
from jax import lax
from jax.experimental import pallas as pl
from jax.experimental.pallas import tpu as pltpu
from jax.sharding import Mesh, PartitionSpec as P

CTX = ("z", "y", "xh")
RING = ("xh", "xl")
F32, BF16 = jnp.float32, jnp.bfloat16
TOK = 256
WIDE = 8


VM = pl.BlockSpec(memory_space=pltpu.VMEM)
SM = pl.BlockSpec(memory_space=pltpu.SMEM)
MIB = 1024 * 1024


def params(mib):
    return pltpu.CompilerParams(vmem_limit_bytes=mib * MIB)


def featurize_kernel(width, x_ref, w_ref, prod_ref, gate_ref, edge_ref):
    tok, chans = x_ref.shape[1:]
    edge_ref[...] = x_ref[:, 0:8, :].astype(F32)

    def one(i, at):
        x = x_ref[i, :, at].astype(F32)
        x1 = pltpu.roll(x, 1, 0)
        x2 = pltpu.roll(x, 2, 0)
        taps = w_ref[i, :, at]
        mix = x2 * taps[0:1] + x1 * taps[1:2] + x * taps[2:3]
        return mix.astype(BF16).astype(F32)

    for c in range(chans // width):
        at = slice(c * width, (c + 1) * width)
        prod_ref[at, :] = (one(1, at) * one(2, at)).T.astype(BF16)
        gate_ref[at, :] = one(0, at).T.astype(BF16)


def featurize(features, taps):
    _, tok, chans = features.shape
    out = jax.ShapeDtypeStruct((chans, tok), BF16)
    return pl.pallas_call(
        functools.partial(featurize_kernel, 256),
        in_specs=[VM, VM],
        out_specs=[VM, VM, VM],
        out_shape=[out, out, jax.ShapeDtypeStruct((3, 8, chans), F32)],
        compiler_params=params(16),
        cost_estimate=pl.CostEstimate(flops=20 * MIB, bytes_accessed=8 * MIB, transcendentals=0),
        name="featurize",
    )(features, taps)


def join_kernel(live_ref, prod_in, gate_in, edge_ref, halo_ref, w_ref, prod_ref, gate_ref):
    live = live_ref[0] != 0
    lanes = 128
    chans = edge_ref.shape[2]
    lane = lax.broadcasted_iota(jnp.int32, (chans, lanes), 1)
    fresh = []
    for i in range(3):
        halo = jnp.where(live, halo_ref[i].astype(F32), 0.0)
        taps, edge = w_ref[i], edge_ref[i]
        row0 = halo[0:1] * taps[0:1] + halo[1:2] * taps[1:2] + edge[0:1] * taps[2:3]
        row1 = halo[1:2] * taps[0:1] + edge[0:1] * taps[1:2] + edge[1:2] * taps[2:3]
        fresh.append(jnp.concatenate([row0, row1], 0).astype(BF16).astype(F32))
    blank = jnp.zeros((lanes - 2, chans), F32)
    for value, old, new in ((fresh[1] * fresh[2], prod_in, prod_ref), (fresh[0], gate_in, gate_ref)):
        first = jnp.concatenate([value, blank], 0).T
        new[:, 0:lanes] = jnp.where(lane < 2, first, old[:, 0:lanes].astype(F32)).astype(BF16)
        new[:, lanes:] = old[:, lanes:]


def join(live, product, gate, edge, halo, taps):
    return pl.pallas_call(
        join_kernel,
        in_specs=[SM] + [VM] * 5,
        out_specs=[VM, VM],
        out_shape=[jax.ShapeDtypeStruct(x.shape, x.dtype) for x in (product, gate)],
        compiler_params=params(8),
        name="join",
    )(live, product, gate, edge, halo, taps)


def toeplitz_kernel(h_ref, t_ref):
    groups, blocks = t_ref.shape[:2]
    span, strip = TOK * WIDE, 16

    def chunk(n, carry):
        g, s = n // (blocks // WIDE), n % (blocks // WIDE)
        lags = h_ref[g, :, pl.ds(pl.multiple_of(s * span, span), span + TOK)]
        wide = jnp.broadcast_to(lags, (strip, span + TOK))
        for i in range(TOK // strip):
            slid = pltpu.roll(wide, i * strip, 1, stride=1, stride_axis=0).astype(BF16)
            for k in range(WIDE):
                t_ref[g, s * WIDE + k, i * strip : (i + 1) * strip, :] = slid[:, (k + 1) * TOK : (k + 2) * TOK]
        return carry

    lax.fori_loop(0, groups * (blocks // WIDE), chunk, 0)


def toeplitz(filters):
    groups, _, length = filters.shape
    blocks = length // TOK - 1
    return pl.pallas_call(
        toeplitz_kernel,
        in_specs=[VM],
        out_specs=VM,
        out_shape=jax.ShapeDtypeStruct((groups, blocks, TOK, TOK), BF16),
        compiler_params=params(8),
        cost_estimate=pl.CostEstimate(flops=0, bytes_accessed=36 * MIB, transcendentals=0),
        name="toeplitz",
    )(filters)


def conv_kernel(x_ref, t_ref, y_ref, wide_ref, acc_ref):
    blocks = x_ref.shape[0]
    groups = t_ref.shape[0]
    per_group = x_ref.shape[1] // groups
    rows = blocks * per_group
    for g in range(groups):
        own = slice(g * per_group, (g + 1) * per_group)
        x = x_ref[:, own, :].reshape(rows, TOK)
        for j in range(WIDE):
            lead = j * per_group
            if lead:
                wide_ref[0:lead, j * TOK : (j + 1) * TOK] = jnp.zeros((lead, TOK), BF16)
            wide_ref[lead:, j * TOK : (j + 1) * TOK] = x[: rows - lead]
        for s in range(blocks // WIDE):
            lead = s * WIDE * per_group
            t = t_ref[g, s * WIDE : (s + 1) * WIDE].reshape(WIDE * TOK, TOK)
            part = jnp.dot(wide_ref[0 : rows - lead, :], t, preferred_element_type=F32)
            if s == 0:
                acc_ref[...] = part
            else:
                acc_ref[lead:, :] += part
        y_ref[:, own, :] = acc_ref[...].astype(BF16).reshape(blocks, per_group, TOK)


def long_conv(x, t):
    blocks, chans, tok = x.shape
    per_group = chans // t.shape[0]
    return pl.pallas_call(
        conv_kernel,
        in_specs=[VM, VM],
        out_specs=VM,
        out_shape=jax.ShapeDtypeStruct(x.shape, BF16),
        scratch_shapes=[
            pltpu.VMEM((blocks * per_group, WIDE * TOK), BF16),
            pltpu.VMEM((blocks * per_group, TOK), F32),
        ],
        compiler_params=params(14),
        cost_estimate=pl.CostEstimate(
            flops=chans * blocks * blocks * tok * tok, bytes_accessed=20 * MIB, transcendentals=0
        ),
        name="long_conv",
    )(x, t)


def gate_kernel(half_ref, conv_ref, near_ref, far_ref, out_ref):
    srcs, _, chans, tok = conv_ref.shape
    group = 8
    half = half_ref[0]
    for r in range(2):
        for c in range(srcs // group):
            some = slice(c * group, (c + 1) * group)
            conv = conv_ref[some, half if r == 0 else 1 - half].astype(F32)
            gate = near_ref[some, half] if r == 0 else far_ref[some]
            gated = (conv * gate.astype(F32)).astype(BF16).astype(F32)
            gated = gated.reshape(group * chans, tok).T.astype(BF16)
            out_ref[r * tok : (r + 1) * tok, c * group * chans : (c + 1) * group * chans] = gated


def gating(half, conv, near, far):
    srcs, halves, chans, tok = conv.shape
    return pl.pallas_call(
        gate_kernel,
        in_specs=[SM, VM, VM, VM],
        out_specs=VM,
        out_shape=jax.ShapeDtypeStruct((halves * tok, srcs * chans), BF16),
        compiler_params=params(8),
        name="gating",
    )(half, conv, near, far)


def project_kernel(own_ref, other_ref, w_ref, out_ref, acc_ref):
    step = pl.program_id(0)
    srcs, _, _, deep, width = w_ref.shape
    w = w_ref[...].reshape(srcs, 2, deep, width)
    part = jnp.dot(own_ref[...], w[:, 0].reshape(srcs * deep, width), preferred_element_type=F32)
    part += jnp.dot(other_ref[...], w[:, 1].reshape(srcs * deep, width), preferred_element_type=F32)

    @pl.when(step == 0)
    def _():
        acc_ref[...] = part

    @pl.when(step != 0)
    def _():
        acc_ref[...] += part

    @pl.when(step == pl.num_programs(0) - 1)
    def _():
        out_ref[...] = acc_ref[...].astype(BF16)


def project(lane, own, other, weights):
    tok, chans = own.shape
    srcs, _, _, deep, width = weights.shape
    steps = 2
    many = srcs // steps
    side = pl.BlockSpec((tok, many * deep), lambda s: (0, s))
    return pl.pallas_call(
        project_kernel,
        grid=(steps,),
        in_specs=[side, side, pl.BlockSpec((many, 1, 2, deep, width), lambda s: (s, lane, 0, 0, 0))],
        out_specs=pl.BlockSpec((tok, width), lambda s: (0, 0)),
        out_shape=jax.ShapeDtypeStruct((tok, width), BF16),
        scratch_shapes=[pltpu.VMEM((tok, width), F32)],
        compiler_params=params(24),
        name="project",
    )(own, other, weights)


def swap(x, axis):
    return lax.ppermute(x, axis, [(0, 1), (1, 0)])


def on_device(features, short_weight, filters, out_weight):
    tok, chans = features.shape[1:]
    deep, wide = out_weight.shape
    xh, xl, core = lax.axis_index("xh"), lax.axis_index("xl"), lax.axis_index("core")
    pick = functools.partial(lax.dynamic_index_in_dim, keepdims=False)

    def columns(lane, core):
        return lax.dynamic_slice_in_dim(out_weight, (lane * 2 + core) * (wide // 4), wide // 4, 1)

    given = swap(jnp.stack([columns(xl, 1 - core), columns(1 - xl, 1 - core)]), "core")
    rows = jnp.stack([columns(xl, core), given[0], columns(1 - xl, core), given[1]])
    weights = lax.all_gather(rows.reshape(2, 2, deep, wide // 4), ("z", "y"), axis=0)

    rim = features[:, tok - 2 :, :]
    ctx_size = lax.axis_size(CTX)
    halo = lax.ppermute(rim, CTX, [(i, (i + 1) % ctx_size) for i in range(ctx_size)])
    live = jnp.where(lax.axis_index(CTX) == 0, 0, 1).astype(jnp.int32)[None]
    product, gate, edge = featurize(features, short_weight)
    product, gate = join(live, product, gate, edge, halo, short_weight)
    mine = chans // ctx_size
    series = lax.all_to_all(
        product.reshape(ctx_size, mine, tok), CTX, split_axis=0, concat_axis=0, tiled=True
    )
    padded = jnp.pad(filters, ((0, 0), (TOK, 0)))[:, None, :]
    gate = gate.reshape(ctx_size // 2, 2, mine, tok)
    far_gate = swap(pick(gate, 1 - xh, 1), "xh")

    series, padded, far_gate = lax.optimization_barrier((series, padded, far_gate))
    convolved = long_conv(series, toeplitz(padded))
    convolved = convolved.reshape(ctx_size // 2, 2, mine, tok)
    back = lax.all_to_all(convolved, ("z", "y"), split_axis=0, concat_axis=0, tiled=True)
    own = gating(xh.astype(jnp.int32)[None], back, gate, far_gate)
    other = swap(own, "core")

    flat = [(0, 1), (1, 0), (2, 3), (3, 2)]
    cross = [(0, 3), (3, 0), (1, 2), (2, 1)]
    mid = tok // 2
    ends = project(0, own, other, weights)
    up = lax.ppermute(ends[tok : tok + mid], RING, flat)
    down = lax.ppermute(ends[tok + mid :], RING, cross)
    sides = project(1, own, other, weights)
    flat_near = lax.ppermute(sides[:mid], RING, flat)
    cross_near = lax.ppermute(sides[tok + mid :], RING, cross)
    flat_far = (sides[mid:tok].astype(F32) + down.astype(F32)).astype(BF16)
    cross_far = (sides[tok : tok + mid].astype(F32) + up.astype(F32)).astype(BF16)
    flat_far = lax.ppermute(flat_far, RING, flat)
    cross_far = lax.ppermute(cross_far, RING, cross)
    total = ends[:tok].astype(F32)
    total = total + jnp.concatenate([flat_near, flat_far]).astype(F32)
    total = total + jnp.concatenate([cross_far, cross_near]).astype(F32)
    return total.astype(BF16)


def solution(mesh):
    fine = Mesh(mesh.devices.reshape(8, 4, 2, 2, 2), ("z", "y", "xh", "xl", "core"))
    tp = ("xl", "core")
    in_specs = (
        P(None, CTX, tp),
        P(None, None, tp),
        P(tp + CTX, None),
        P(tp + CTX, None),
    )
    return jax.shard_map(
        on_device, mesh=fine, in_specs=in_specs, out_specs=P(CTX, tp), check_vma=False
    )
```

```python
import functools

import jax
import jax.numpy as jnp
from jax import lax
from jax.experimental import pallas as pl
from jax.experimental.pallas import tpu as pltpu
from jax.sharding import Mesh, PartitionSpec as P

CTX = ("z", "y", "xh")
RING = ("xh", "xl")
F32, BF16 = jnp.float32, jnp.bfloat16
TOK = 256
WIDE = 8


VM = pl.BlockSpec(memory_space=pltpu.VMEM)
SM = pl.BlockSpec(memory_space=pltpu.SMEM)
MIB = 1024 * 1024


def params(mib):
    return pltpu.CompilerParams(vmem_limit_bytes=mib * MIB)


def featurize_kernel(width, x_ref, w_ref, prod_ref, gate_ref, edge_ref):
    tok, chans = x_ref.shape[1:]
    edge_ref[...] = x_ref[:, 0:8, :].astype(F32)

    def one(i, at):
        x = x_ref[i, :, at].astype(F32)
        x1 = pltpu.roll(x, 1, 0)
        x2 = pltpu.roll(x, 2, 0)
        taps = w_ref[i, :, at]
        mix = x2 * taps[0:1] + x1 * taps[1:2] + x * taps[2:3]
        return mix.astype(BF16).astype(F32)

    for c in range(chans // width):
        at = slice(c * width, (c + 1) * width)
        prod_ref[at, :] = (one(1, at) * one(2, at)).T.astype(BF16)
        gate_ref[at, :] = one(0, at).T.astype(BF16)


def featurize(features, taps):
    _, tok, chans = features.shape
    out = jax.ShapeDtypeStruct((chans, tok), BF16)
    return pl.pallas_call(
        functools.partial(featurize_kernel, 256),
        in_specs=[VM, VM],
        out_specs=[VM, VM, VM],
        out_shape=[out, out, jax.ShapeDtypeStruct((3, 8, chans), F32)],
        compiler_params=params(16),
        cost_estimate=pl.CostEstimate(flops=20 * MIB, bytes_accessed=8 * MIB, transcendentals=0),
        name="featurize",
    )(features, taps)


def join_kernel(live_ref, prod_in, gate_in, edge_ref, halo_ref, w_ref, prod_ref, gate_ref):
    live = live_ref[0] != 0
    lanes = 128
    chans = edge_ref.shape[2]
    lane = lax.broadcasted_iota(jnp.int32, (chans, lanes), 1)
    fresh = []
    for i in range(3):
        halo = jnp.where(live, halo_ref[i].astype(F32), 0.0)
        taps, edge = w_ref[i], edge_ref[i]
        row0 = halo[0:1] * taps[0:1] + halo[1:2] * taps[1:2] + edge[0:1] * taps[2:3]
        row1 = halo[1:2] * taps[0:1] + edge[0:1] * taps[1:2] + edge[1:2] * taps[2:3]
        fresh.append(jnp.concatenate([row0, row1], 0).astype(BF16).astype(F32))
    blank = jnp.zeros((lanes - 2, chans), F32)
    for value, old, new in ((fresh[1] * fresh[2], prod_in, prod_ref), (fresh[0], gate_in, gate_ref)):
        first = jnp.concatenate([value, blank], 0).T
        new[:, 0:lanes] = jnp.where(lane < 2, first, old[:, 0:lanes].astype(F32)).astype(BF16)
        new[:, lanes:] = old[:, lanes:]


def join(live, product, gate, edge, halo, taps):
    return pl.pallas_call(
        join_kernel,
        in_specs=[SM] + [VM] * 5,
        out_specs=[VM, VM],
        out_shape=[jax.ShapeDtypeStruct(x.shape, x.dtype) for x in (product, gate)],
        compiler_params=params(8),
        name="join",
    )(live, product, gate, edge, halo, taps)


def toeplitz_kernel(h_ref, t_ref):
    groups, blocks = t_ref.shape[:2]
    span, strip = TOK * WIDE, 16

    def chunk(n, carry):
        g, s = n // (blocks // WIDE), n % (blocks // WIDE)
        lags = h_ref[g, :, pl.ds(pl.multiple_of(s * span, span), span + TOK)]
        wide = jnp.broadcast_to(lags, (strip, span + TOK))
        for i in range(TOK // strip):
            slid = pltpu.roll(wide, i * strip, 1, stride=1, stride_axis=0).astype(BF16)
            for k in range(WIDE):
                t_ref[g, s * WIDE + k, i * strip : (i + 1) * strip, :] = slid[:, (k + 1) * TOK : (k + 2) * TOK]
        return carry

    lax.fori_loop(0, groups * (blocks // WIDE), chunk, 0)


def toeplitz(filters):
    groups, _, length = filters.shape
    blocks = length // TOK - 1
    return pl.pallas_call(
        toeplitz_kernel,
        in_specs=[VM],
        out_specs=VM,
        out_shape=jax.ShapeDtypeStruct((groups, blocks, TOK, TOK), BF16),
        compiler_params=params(8),
        cost_estimate=pl.CostEstimate(flops=0, bytes_accessed=36 * MIB, transcendentals=0),
        name="toeplitz",
    )(filters)


def conv_kernel(x_ref, t_ref, y_ref, wide_ref, acc_ref):
    blocks = x_ref.shape[0]
    groups = t_ref.shape[0]
    per_group = x_ref.shape[1] // groups
    rows = blocks * per_group
    for g in range(groups):
        own = slice(g * per_group, (g + 1) * per_group)
        x = x_ref[:, own, :].reshape(rows, TOK)
        for j in range(WIDE):
            lead = j * per_group
            if lead:
                wide_ref[0:lead, j * TOK : (j + 1) * TOK] = jnp.zeros((lead, TOK), BF16)
            wide_ref[lead:, j * TOK : (j + 1) * TOK] = x[: rows - lead]
        for s in range(blocks // WIDE):
            lead = s * WIDE * per_group
            t = t_ref[g, s * WIDE : (s + 1) * WIDE].reshape(WIDE * TOK, TOK)
            part = jnp.dot(wide_ref[0 : rows - lead, :], t, preferred_element_type=F32)
            if s == 0:
                acc_ref[...] = part
            else:
                acc_ref[lead:, :] += part
        y_ref[:, own, :] = acc_ref[...].astype(BF16).reshape(blocks, per_group, TOK)


def long_conv(x, t):
    blocks, chans, tok = x.shape
    per_group = chans // t.shape[0]
    return pl.pallas_call(
        conv_kernel,
        in_specs=[VM, VM],
        out_specs=VM,
        out_shape=jax.ShapeDtypeStruct(x.shape, BF16),
        scratch_shapes=[
            pltpu.VMEM((blocks * per_group, WIDE * TOK), BF16),
            pltpu.VMEM((blocks * per_group, TOK), F32),
        ],
        compiler_params=params(14),
        cost_estimate=pl.CostEstimate(
            flops=chans * blocks * blocks * tok * tok, bytes_accessed=20 * MIB, transcendentals=0
        ),
        name="long_conv",
    )(x, t)


def gate_kernel(half_ref, conv_ref, near_ref, far_ref, out_ref):
    srcs, _, chans, tok = conv_ref.shape
    group = 8
    half = half_ref[0]
    for r in range(2):
        for c in range(srcs // group):
            some = slice(c * group, (c + 1) * group)
            conv = conv_ref[some, half if r == 0 else 1 - half].astype(F32)
            gate = near_ref[some, half] if r == 0 else far_ref[some]
            gated = (conv * gate.astype(F32)).astype(BF16).astype(F32)
            gated = gated.reshape(group * chans, tok).T.astype(BF16)
            out_ref[r * tok : (r + 1) * tok, c * group * chans : (c + 1) * group * chans] = gated


def gating(half, conv, near, far):
    srcs, halves, chans, tok = conv.shape
    return pl.pallas_call(
        gate_kernel,
        in_specs=[SM, VM, VM, VM],
        out_specs=VM,
        out_shape=jax.ShapeDtypeStruct((halves * tok, srcs * chans), BF16),
        compiler_params=params(8),
        name="gating",
    )(half, conv, near, far)


def project_kernel(rows, lane, own_ref, other_ref, w_ref, *out_refs):
    srcs, _, _, deep, width = w_ref.shape
    part = None
    for c, side_ref in enumerate((own_ref, other_ref)):
        w = w_ref[:, lane, c].reshape(srcs * deep, width)
        term = jnp.dot(side_ref[rows, :], w, preferred_element_type=F32)
        part = term if part is None else part + term
    tall = out_refs[0].shape[0]
    for n, out_ref in enumerate(out_refs):
        out_ref[...] = part[n * tall : (n + 1) * tall].astype(out_ref.dtype)


def project(rows, lane, pieces, own, other, weights, out_type=BF16):
    srcs, _, _, deep, width = weights.shape
    tok = rows.stop - rows.start
    return pl.pallas_call(
        functools.partial(project_kernel, rows, lane),
        in_specs=[VM, VM, VM],
        out_specs=[VM] * pieces,
        out_shape=[jax.ShapeDtypeStruct((tok // pieces, width), out_type)] * pieces,
        compiler_params=params(16),
        cost_estimate=pl.CostEstimate(
            flops=4 * tok * srcs * deep * width, bytes_accessed=6 * MIB, transcendentals=0
        ),
        name="project",
    )(own, other, weights)


def swap(x, axis):
    return lax.ppermute(x, axis, [(0, 1), (1, 0)])


def on_device(features, short_weight, filters, out_weight):
    tok, chans = features.shape[1:]
    deep, wide = out_weight.shape
    xh, xl, core = lax.axis_index("xh"), lax.axis_index("xl"), lax.axis_index("core")
    pick = functools.partial(lax.dynamic_index_in_dim, keepdims=False)

    def columns(lane, core):
        return lax.dynamic_slice_in_dim(out_weight, (lane * 2 + core) * (wide // 4), wide // 4, 1)

    given = swap(jnp.stack([columns(xl, 1 - core), columns(1 - xl, 1 - core)]), "core")
    rows = jnp.stack([columns(xl, core), given[0], columns(1 - xl, core), given[1]])
    weights = lax.all_gather(rows.reshape(2, 2, deep, wide // 4), ("z", "y"), axis=0)

    rim = features[:, tok - 2 :, :]
    ctx_size = lax.axis_size(CTX)
    halo = lax.ppermute(rim, CTX, [(i, (i + 1) % ctx_size) for i in range(ctx_size)])
    live = jnp.where(lax.axis_index(CTX) == 0, 0, 1).astype(jnp.int32)[None]
    product, gate, edge = featurize(features, short_weight)
    product, gate = join(live, product, gate, edge, halo, short_weight)
    mine = chans // ctx_size
    series = lax.all_to_all(
        product.reshape(ctx_size, mine, tok), CTX, split_axis=0, concat_axis=0, tiled=True
    )
    padded = jnp.pad(filters, ((0, 0), (TOK, 0)))[:, None, :]
    gate = gate.reshape(ctx_size // 2, 2, mine, tok)
    far_gate = swap(pick(gate, 1 - xh, 1), "xh")

    series, padded, far_gate = lax.optimization_barrier((series, padded, far_gate))
    convolved = long_conv(series, toeplitz(padded))
    convolved = convolved.reshape(ctx_size // 2, 2, mine, tok)
    back = lax.all_to_all(convolved, ("z", "y"), split_axis=0, concat_axis=0, tiled=True)
    own = gating(xh.astype(jnp.int32)[None], back, gate, far_gate)
    other = swap(own, "core")

    flat = [(0, 1), (1, 0), (2, 3), (3, 2)]
    cross = [(0, 3), (3, 0), (1, 2), (2, 1)]
    whole = (own, other, weights)
    ahead = project(slice(tok, 2 * tok), 0, 2, *whole)
    up = lax.ppermute(ahead[0], RING, flat)
    down = lax.ppermute(ahead[1], RING, cross)
    sides = project(slice(0, 2 * tok), 1, 4, *whole)
    flat_near = lax.ppermute(sides[0], RING, flat)
    cross_near = lax.ppermute(sides[3], RING, cross)
    flat_far = (sides[1].astype(F32) + down.astype(F32)).astype(BF16)
    cross_far = (sides[2].astype(F32) + up.astype(F32)).astype(BF16)
    flat_far = lax.ppermute(flat_far, RING, flat)
    cross_far = lax.ppermute(cross_far, RING, cross)
    (total,) = project(slice(0, tok), 0, 1, *whole, F32)
    total = total + jnp.concatenate([flat_near, flat_far]).astype(F32)
    total = total + jnp.concatenate([cross_far, cross_near]).astype(F32)
    return total.astype(BF16)


def solution(mesh):
    fine = Mesh(mesh.devices.reshape(8, 4, 2, 2, 2), ("z", "y", "xh", "xl", "core"))
    tp = ("xl", "core")
    in_specs = (
        P(None, CTX, tp),
        P(None, None, tp),
        P(tp + CTX, None),
        P(tp + CTX, None),
    )
    return jax.shard_map(
        on_device, mesh=fine, in_specs=in_specs, out_specs=P(CTX, tp), check_vma=False
    )
```

```python
import functools

import jax
import jax.numpy as jnp
from jax import lax
from jax.experimental import pallas as pl
from jax.experimental.pallas import tpu as pltpu
from jax.sharding import Mesh, PartitionSpec as P

CTX = ("z", "y", "xh")
RING = ("xh", "xl")
F32, BF16 = jnp.float32, jnp.bfloat16
TOK = 256
WIDE = 8


VM = pl.BlockSpec(memory_space=pltpu.VMEM)
SM = pl.BlockSpec(memory_space=pltpu.SMEM)
MIB = 1024 * 1024


def params(mib):
    return pltpu.CompilerParams(vmem_limit_bytes=mib * MIB)


def featurize_kernel(width, x_ref, w_ref, prod_ref, gate_ref, edge_ref):
    tok, chans = x_ref.shape[1:]
    edge_ref[...] = x_ref[:, 0:8, :].astype(F32)

    def one(i, at):
        x = x_ref[i, :, at].astype(F32)
        x1 = pltpu.roll(x, 1, 0)
        x2 = pltpu.roll(x, 2, 0)
        taps = w_ref[i, :, at]
        mix = x2 * taps[0:1] + x1 * taps[1:2] + x * taps[2:3]
        return mix.astype(BF16).astype(F32)

    for c in range(chans // width):
        at = slice(c * width, (c + 1) * width)
        prod_ref[at, :] = (one(1, at) * one(2, at)).T.astype(BF16)
        gate_ref[at, :] = one(0, at).T.astype(BF16)


def featurize(features, taps):
    _, tok, chans = features.shape
    out = jax.ShapeDtypeStruct((chans, tok), BF16)
    return pl.pallas_call(
        functools.partial(featurize_kernel, 256),
        in_specs=[VM, VM],
        out_specs=[VM, VM, VM],
        out_shape=[out, out, jax.ShapeDtypeStruct((3, 8, chans), F32)],
        compiler_params=params(16),
        cost_estimate=pl.CostEstimate(flops=20 * MIB, bytes_accessed=8 * MIB, transcendentals=0),
        name="featurize",
    )(features, taps)


def join_kernel(live_ref, prod_in, gate_in, edge_ref, halo_ref, w_ref, prod_ref, gate_ref):
    live = live_ref[0] != 0
    lanes = 128
    chans = edge_ref.shape[2]
    lane = lax.broadcasted_iota(jnp.int32, (chans, lanes), 1)
    fresh = []
    for i in range(3):
        halo = jnp.where(live, halo_ref[i].astype(F32), 0.0)
        taps, edge = w_ref[i], edge_ref[i]
        row0 = halo[0:1] * taps[0:1] + halo[1:2] * taps[1:2] + edge[0:1] * taps[2:3]
        row1 = halo[1:2] * taps[0:1] + edge[0:1] * taps[1:2] + edge[1:2] * taps[2:3]
        fresh.append(jnp.concatenate([row0, row1], 0).astype(BF16).astype(F32))
    blank = jnp.zeros((lanes - 2, chans), F32)
    for value, old, new in ((fresh[1] * fresh[2], prod_in, prod_ref), (fresh[0], gate_in, gate_ref)):
        first = jnp.concatenate([value, blank], 0).T
        new[:, 0:lanes] = jnp.where(lane < 2, first, old[:, 0:lanes].astype(F32)).astype(BF16)
        new[:, lanes:] = old[:, lanes:]


def join(live, product, gate, edge, halo, taps):
    return pl.pallas_call(
        join_kernel,
        in_specs=[SM] + [VM] * 5,
        out_specs=[VM, VM],
        out_shape=[jax.ShapeDtypeStruct(x.shape, x.dtype) for x in (product, gate)],
        compiler_params=params(8),
        name="join",
    )(live, product, gate, edge, halo, taps)


def toeplitz_kernel(h_ref, t_ref):
    groups, blocks = t_ref.shape[:2]
    span, strip = TOK * WIDE, 16

    def chunk(n, carry):
        g, s = n // (blocks // WIDE), n % (blocks // WIDE)
        lags = h_ref[g, :, pl.ds(pl.multiple_of(s * span, span), span + TOK)]
        wide = jnp.broadcast_to(lags, (strip, span + TOK))
        for i in range(TOK // strip):
            slid = pltpu.roll(wide, i * strip, 1, stride=1, stride_axis=0).astype(BF16)
            for k in range(WIDE):
                t_ref[g, s * WIDE + k, i * strip : (i + 1) * strip, :] = slid[:, (k + 1) * TOK : (k + 2) * TOK]
        return carry

    lax.fori_loop(0, groups * (blocks // WIDE), chunk, 0)


def toeplitz(filters):
    groups, _, length = filters.shape
    blocks = length // TOK - 1
    return pl.pallas_call(
        toeplitz_kernel,
        in_specs=[VM],
        out_specs=VM,
        out_shape=jax.ShapeDtypeStruct((groups, blocks, TOK, TOK), BF16),
        compiler_params=params(8),
        cost_estimate=pl.CostEstimate(flops=0, bytes_accessed=36 * MIB, transcendentals=0),
        name="toeplitz",
    )(filters)


def conv_kernel(x_ref, t_ref, y_ref, wide_ref, acc_ref):
    blocks = x_ref.shape[0]
    groups = t_ref.shape[0]
    per_group = x_ref.shape[1] // groups
    rows = blocks * per_group
    for g in range(groups):
        own = slice(g * per_group, (g + 1) * per_group)
        x = x_ref[:, own, :].reshape(rows, TOK)
        for j in range(WIDE):
            lead = j * per_group
            if lead:
                wide_ref[0:lead, j * TOK : (j + 1) * TOK] = jnp.zeros((lead, TOK), BF16)
            wide_ref[lead:, j * TOK : (j + 1) * TOK] = x[: rows - lead]
        for s in range(blocks // WIDE):
            lead = s * WIDE * per_group
            t = t_ref[g, s * WIDE : (s + 1) * WIDE].reshape(WIDE * TOK, TOK)
            part = jnp.dot(wide_ref[0 : rows - lead, :], t, preferred_element_type=F32)
            if s == 0:
                acc_ref[...] = part
            else:
                acc_ref[lead:, :] += part
        y_ref[:, own, :] = acc_ref[...].astype(BF16).reshape(blocks, per_group, TOK)


def long_conv(x, t):
    blocks, chans, tok = x.shape
    per_group = chans // t.shape[0]
    return pl.pallas_call(
        conv_kernel,
        in_specs=[VM, VM],
        out_specs=VM,
        out_shape=jax.ShapeDtypeStruct(x.shape, BF16),
        scratch_shapes=[
            pltpu.VMEM((blocks * per_group, WIDE * TOK), BF16),
            pltpu.VMEM((blocks * per_group, TOK), F32),
        ],
        compiler_params=params(14),
        cost_estimate=pl.CostEstimate(
            flops=chans * blocks * blocks * tok * tok, bytes_accessed=20 * MIB, transcendentals=0
        ),
        name="long_conv",
    )(x, t)


def gate_kernel(half_ref, conv_ref, near_ref, far_ref, out_ref):
    srcs, _, chans, tok = conv_ref.shape
    group = 8
    half = half_ref[0]
    for r in range(2):
        for c in range(srcs // group):
            parts = []
            for d in range(group):
                src = d * (srcs // group) + c
                conv = conv_ref[src, half if r == 0 else 1 - half].astype(F32)
                gate = near_ref[src, half] if r == 0 else far_ref[src]
                parts.append((conv * gate.astype(F32)).astype(BF16).astype(F32))
            gated = jnp.concatenate(parts, 0).T.astype(BF16)
            out_ref[r * tok : (r + 1) * tok, c * group * chans : (c + 1) * group * chans] = gated


def gating(half, conv, near, far):
    srcs, halves, chans, tok = conv.shape
    return pl.pallas_call(
        gate_kernel,
        in_specs=[SM, VM, VM, VM],
        out_specs=VM,
        out_shape=jax.ShapeDtypeStruct((halves * tok, srcs * chans), BF16),
        compiler_params=params(8),
        name="gating",
    )(half, conv, near, far)


def project_kernel(rows, lane, own_ref, other_ref, w_ref, *out_refs):
    srcs, _, _, deep, width = w_ref.shape
    part = None
    for c, side_ref in enumerate((own_ref, other_ref)):
        w = w_ref[:, lane, c].reshape(srcs * deep, width)
        term = jnp.dot(side_ref[rows, :], w, preferred_element_type=F32)
        part = term if part is None else part + term
    tall = out_refs[0].shape[0]
    for n, out_ref in enumerate(out_refs):
        out_ref[...] = part[n * tall : (n + 1) * tall].astype(out_ref.dtype)


def project(rows, lane, pieces, own, other, weights, out_type=BF16):
    srcs, _, _, deep, width = weights.shape
    tok = rows.stop - rows.start
    return pl.pallas_call(
        functools.partial(project_kernel, rows, lane),
        in_specs=[VM, VM, VM],
        out_specs=[VM] * pieces,
        out_shape=[jax.ShapeDtypeStruct((tok // pieces, width), out_type)] * pieces,
        compiler_params=params(16),
        cost_estimate=pl.CostEstimate(
            flops=4 * tok * srcs * deep * width, bytes_accessed=6 * MIB, transcendentals=0
        ),
        name="project",
    )(own, other, weights)


def swap(x, axis):
    return lax.ppermute(x, axis, [(0, 1), (1, 0)])


def on_device(features, short_weight, filters, out_weight):
    tok, chans = features.shape[1:]
    deep, wide = out_weight.shape
    xh, xl, core = lax.axis_index("xh"), lax.axis_index("xl"), lax.axis_index("core")
    pick = functools.partial(lax.dynamic_index_in_dim, keepdims=False)

    def columns(weight, lane):
        return lax.dynamic_slice_in_dim(weight, (lane * 2 + core) * (wide // 4), wide // 4, 1)

    given = swap(out_weight, "core")
    rows = jnp.stack([columns(w, lane) for lane in (xl, 1 - xl) for w in (out_weight, given)])
    weights = lax.all_gather(rows.reshape(2, 2, deep, wide // 4), ("y", "z"), axis=0)

    rim = features[:, tok - 2 :, :]
    ctx_size = lax.axis_size(CTX)
    halo = lax.ppermute(rim, CTX, [(i, (i + 1) % ctx_size) for i in range(ctx_size)])
    live = jnp.where(lax.axis_index(CTX) == 0, 0, 1).astype(jnp.int32)[None]
    product, gate, edge = featurize(features, short_weight)
    product, gate = join(live, product, gate, edge, halo, short_weight)
    mine = chans // ctx_size
    series = lax.all_to_all(
        product.reshape(ctx_size, mine, tok), CTX, split_axis=0, concat_axis=0, tiled=True
    )
    padded = jnp.pad(filters, ((0, 0), (TOK, 0)))[:, None, :]
    gate = gate.reshape(ctx_size // 2, 2, mine, tok)
    far_gate = swap(pick(gate, 1 - xh, 1), "xh")

    series, padded, far_gate = lax.optimization_barrier((series, padded, far_gate))
    convolved = long_conv(series, toeplitz(padded))
    convolved = convolved.reshape(ctx_size // 2, 2, mine, tok)
    back = lax.all_to_all(convolved, ("z", "y"), split_axis=0, concat_axis=0, tiled=True)
    own = gating(xh.astype(jnp.int32)[None], back, gate, far_gate)
    other = swap(own, "core")

    flat = [(0, 1), (1, 0), (2, 3), (3, 2)]
    cross = [(0, 3), (3, 0), (1, 2), (2, 1)]
    whole = (own, other, weights)
    ahead = project(slice(tok, 2 * tok), 0, 2, *whole)
    up = lax.ppermute(ahead[0], RING, flat)
    down = lax.ppermute(ahead[1], RING, cross)
    sides = project(slice(0, 2 * tok), 1, 4, *whole)
    flat_near = lax.ppermute(sides[0], RING, flat)
    cross_near = lax.ppermute(sides[3], RING, cross)
    flat_far = (sides[1].astype(F32) + down.astype(F32)).astype(BF16)
    cross_far = (sides[2].astype(F32) + up.astype(F32)).astype(BF16)
    flat_far = lax.ppermute(flat_far, RING, flat)
    cross_far = lax.ppermute(cross_far, RING, cross)
    (total,) = project(slice(0, tok), 0, 1, *whole, F32)
    total = total + jnp.concatenate([flat_near, flat_far]).astype(F32)
    total = total + jnp.concatenate([cross_far, cross_near]).astype(F32)
    return total.astype(BF16)


def solution(mesh):
    fine = Mesh(mesh.devices.reshape(8, 4, 2, 2, 2), ("z", "y", "xh", "xl", "core"))
    tp = ("xl", "core")
    in_specs = (
        P(None, CTX, tp),
        P(None, None, tp),
        P(tp + CTX, None),
        P(tp + CTX, None),
    )
    return jax.shard_map(
        on_device, mesh=fine, in_specs=in_specs, out_specs=P(CTX, tp), check_vma=False
    )
```
